128 devices in a mesh: loader: 8 (over z, core), encoder: 16 (over x, y).
Axes of the slice: x: 4, y: 4, z: 4, core: 2. Of those that a mesh axis runs over, the one named last changes fastest.
Arguments:
- tokens: bfloat16 [98304, 1152], P(('loader', 'encoder')), may hold values from -60 to 60
- lengths: int32 [8, 48], P('loader'), may hold values from 64 to 512, as said below
- norm_gains: float32 [2, 1152], replicated, may hold values from 0.25 to 1.75
- norm_shifts: float32 [2, 1152], replicated, may hold values from -1.5 to 1.5
- qkv_weight: bfloat16 [1152, 3456], replicated, may hold values from -1 to 1
- qkv_bias: float32 [3456], replicated, may hold values from -3 to 3
- out_weight: bfloat16 [1152, 1152], replicated, may hold values from -0.1875 to 0.1875
- out_bias: float32 [1152], replicated, may hold values from -3 to 3
- up_weight: bfloat16 [1152, 4304], P('loader', 'encoder'), may hold values from -0.1875 to 0.1875
- up_bias: float32 [4304], replicated, may hold values from -3 to 3
- down_weight: bfloat16 [4304, 1152], P('encoder', 'loader'), may hold values from -0.09375 to 0.09375
- down_bias: float32 [1152], replicated, may hold values from -3 to 3
Outputs:
- layer_out: bfloat16 [98304, 1152], P(('loader', 'encoder'))
The draws below stay inside these ranges and needn't reach their ends.
Inputs may be any that keep to these rules, and one draw needn't show every extreme that they name: `lengths`: each row's counts add up to 12288 exactly; in each row one image has 512 patches and one has 64.
All inputs are finite; a program needn't handle non-finite values.
Results may differ from the reference program's by a relative error of at most 0.012.
The reference program's roundings to bfloat16 on the way (of `first`, `qkv`, `probs`, `mixed`, `second` and `hidden`) count: a program that leaves them out, or rounds other values in their place, can miss the bound.
Values may be sent and summed in bfloat16 or wider, within the bound.
A program may use at most 128 MiB of HBM per device.

```python
import math
import jax
import jax.numpy as jnp
from jax import lax

D = 1152
HEADS = 16
FF = 4304
MAXLEN = 512
MINLEN = 64
MEANLEN = 256
GROUP_ROWS = 12288
IMG_GRP = 48
TOKENS = 98304
N_LOADER = 8


def draw_tokens(key, part):
    key = jax.random.fold_in(key, 11)
    first_key, row_key, column_key = jax.random.split(key, 3)
    base = jax.random.normal(first_key, (TOKENS, D), jnp.float32)
    row_scale = jnp.exp(jax.random.uniform(row_key, (TOKENS, 1), jnp.float32, math.log(0.3), math.log(3.0)))
    column_scale = jnp.exp(jax.random.uniform(column_key, (1, D), jnp.float32, math.log(0.5), math.log(2.5)))
    values = jnp.clip(base, -6.0, 6.0) * row_scale * column_scale
    return jnp.clip(values, -60.0, 60.0).astype(jnp.bfloat16)


def draw_qkv_weight(key, part):
    key = jax.random.fold_in(key, 23)
    base = jax.random.normal(key, (D, HEADS, 3, D // HEADS), jnp.float32) * D ** (-0.5)
    return jnp.clip(base, -1.0, 1.0).reshape(D, 3 * D).astype(jnp.bfloat16)


def one_group(group_key):
    order_key, move_key = jax.random.split(group_key)
    order = jax.random.permutation(order_key, IMG_GRP)
    reach = min(MEANLEN - MINLEN, MAXLEN - MEANLEN)
    pairs = (IMG_GRP - 3) // 2
    ranked = jnp.full((IMG_GRP,), MEANLEN, jnp.int32)
    ranked = ranked.at[0].set(MAXLEN).at[1].set(MINLEN).at[2].set(3 * MEANLEN - MAXLEN - MINLEN)
    if pairs > 0:
        moves = jax.random.randint(move_key, (pairs,), 0, reach + 1, jnp.int32)
        ranked = ranked.at[3:3 + 2 * pairs:2].add(moves)
        ranked = ranked.at[4:4 + 2 * pairs:2].add(-moves)
    return jnp.zeros((IMG_GRP,), jnp.int32).at[order].set(ranked)


def draw_lengths(key, part):
    key = jax.random.fold_in(key, 37)
    group_keys = jax.random.split(key, N_LOADER)
    return jax.vmap(one_group)(group_keys).astype(jnp.int32)


def levels(key, shape, shards, smallest, high):
    def one(dim, blocks):
        draws = jax.random.uniform(jax.random.fold_in(jax.random.fold_in(key, 6), dim), (blocks,), jnp.float32, smallest / len(shards), high / len(shards))
        return jnp.repeat(jnp.exp(draws), shape[dim] // blocks).reshape((-1,) + (1,) * (len(shape) - dim - 1))

    level = one(*shards[0])
    for cut in shards[1:]:
        level = level * one(*cut)
    return level


def gaussian(own_key, shape, scale, most, cuts=(), kind=jnp.bfloat16):
    factor_of = levels(own_key, shape, cuts, -0.22, 0.18) if cuts else 1.0
    drawn = jax.random.normal(own_key, shape, jnp.float32) * scale * factor_of
    return jnp.minimum(jnp.maximum(drawn, -most), most).astype(kind)


def setup_inputs(seed: int = 0) -> dict:
    key_of = jax.random.split(jax.random.key(seed), 13)
    tokens = draw_tokens(jax.random.fold_in(key_of[12], 71), 0)
    lengths = draw_lengths(jax.random.fold_in(key_of[12], 71), 0)
    norm_gains = jnp.clip(1.0 + 0.15 * jax.random.normal(key_of[2], (2, D), jnp.float32), 0.25, 1.75)
    norm_shifts = gaussian(key_of[3], (2, D), 0.3, 1.5, (), jnp.float32)
    qkv_weight = draw_qkv_weight(jax.random.fold_in(key_of[12], 71), 0)
    qkv_bias = gaussian(key_of[5], (3 * D,), 0.5, 3.0, (), jnp.float32)
    out_weight = gaussian(key_of[6], (D, D), D ** -0.5, 0.1875)
    out_bias = gaussian(key_of[7], (D,), 0.5, 3.0, (), jnp.float32)
    up_weight = gaussian(key_of[8], (D, FF), D ** -0.5, 0.1875, ((0, 8), (1, 16)))
    up_bias = gaussian(key_of[9], (FF,), 0.5, 3.0, (), jnp.float32)
    down_weight = gaussian(key_of[10], (FF, D), FF ** -0.5, 0.09375, ((0, 16), (1, 8)))
    down_bias = gaussian(key_of[11], (D,), 0.5, 3.0, (), jnp.float32)
    return {"tokens": tokens, "lengths": lengths, "norm_gains": norm_gains, "norm_shifts": norm_shifts, "qkv_weight": qkv_weight, "qkv_bias": qkv_bias, "out_weight": out_weight, "out_bias": out_bias, "up_weight": up_weight, "up_bias": up_bias, "down_weight": down_weight, "down_bias": down_bias}


def normalize(values, gain, shift):
    center = values - lax.optimization_barrier(jnp.mean(values, axis=-1, keepdims=True))
    spread = lax.optimization_barrier(jnp.mean(center * center, axis=-1, keepdims=True))
    return center * lax.rsqrt(spread + 1e-06) * gain + shift

def block_size(count):
    for candidate in (512, 256, 128):
        if count % candidate == 0:
            return candidate
    return count

def segment_ids(positions, image_ends, group_total):
    inside = (positions >= 0) & (positions < group_total)
    found = lax.optimization_barrier(jnp.sum((image_ends[None, :] <= positions[:, None]).astype(jnp.int32), axis=1)).astype(jnp.int32)
    return jnp.where(inside, found, jnp.int32(-1)).astype(jnp.int32)

def attend(queries, keys, values, query_ids, key_ids, margin):
    count = queries.shape[0]
    step_rows = block_size(count)
    window = step_rows + 2 * margin
    scale = queries.shape[2] ** (-0.5)

    def per_block(block_index):
        start = (block_index * step_rows).astype(jnp.int32)
        query_block = lax.dynamic_slice_in_dim(queries, start, step_rows, 0).astype(jnp.float32)
        key_block = lax.dynamic_slice_in_dim(keys, start, window, 0).astype(jnp.float32)
        value_block = lax.dynamic_slice_in_dim(values, start, window, 0).astype(jnp.float32)
        query_seg = lax.dynamic_slice_in_dim(query_ids, start, step_rows, 0)
        key_seg = lax.dynamic_slice_in_dim(key_ids, start, window, 0)
        scores = jnp.einsum('qhd,khd->hqk', query_block, key_block) * scale
        same = query_seg[:, None] == key_seg[None, :]
        scores = jnp.where(same[None], scores, -jnp.inf)
        largest = lax.optimization_barrier(jnp.max(scores, axis=-1, keepdims=True))
        weights = jnp.exp(scores - largest)
        probs = (weights / lax.optimization_barrier(jnp.sum(weights, axis=-1, keepdims=True))).astype(jnp.bfloat16)
        result = jnp.einsum('hqk,khd->qhd', probs.astype(jnp.float32), value_block)
        return result.astype(jnp.bfloat16)
    blocks = lax.map(per_block, jnp.arange(count // step_rows, dtype=jnp.int32))
    return blocks.reshape(count, queries.shape[1], queries.shape[2])

def reference(tokens, lengths, norm_gains, norm_shifts, qkv_weight, qkv_bias, out_weight, out_bias, up_weight, up_bias, down_weight, down_bias):
    head_size = D // HEADS

    def group_layer(pair):
        group_tokens, group_lengths = pair
        wide = group_tokens.astype(jnp.float32)
        first = normalize(wide, norm_gains[0], norm_shifts[0]).astype(jnp.bfloat16)
        qkv = (jnp.dot(first, qkv_weight, preferred_element_type=jnp.float32) + qkv_bias).astype(jnp.bfloat16)
        qkv = qkv.reshape(GROUP_ROWS, HEADS, 3, head_size)
        keys = jnp.pad(qkv[:, :, 1], ((MAXLEN, MAXLEN), (0, 0), (0, 0)))
        values = jnp.pad(qkv[:, :, 2], ((MAXLEN, MAXLEN), (0, 0), (0, 0)))
        image_ends = jnp.cumsum(group_lengths, dtype=jnp.int32)
        positions = jnp.arange(GROUP_ROWS, dtype=jnp.int32)
        key_positions = jnp.arange(GROUP_ROWS + 2 * MAXLEN, dtype=jnp.int32) - MAXLEN
        mixed = attend(qkv[:, :, 0], keys, values, segment_ids(positions, image_ends, GROUP_ROWS), segment_ids(key_positions, image_ends, GROUP_ROWS), MAXLEN)
        mixed = mixed.reshape(GROUP_ROWS, D)
        attended = wide + jnp.dot(mixed, out_weight, preferred_element_type=jnp.float32) + out_bias
        second = normalize(attended, norm_gains[1], norm_shifts[1]).astype(jnp.bfloat16)
        hidden = jax.nn.gelu(jnp.dot(second, up_weight, preferred_element_type=jnp.float32) + up_bias, approximate=True).astype(jnp.bfloat16)
        result = attended + jnp.dot(hidden, down_weight, preferred_element_type=jnp.float32) + down_bias
        return result.astype(jnp.bfloat16)
    grouped = tokens.reshape(N_LOADER, GROUP_ROWS, D)
    outputs = lax.map(group_layer, (grouped, lengths))
    return outputs.reshape(TOKENS, D)
```

```python
import functools

import jax
import jax.numpy as jnp
import numpy as np
from jax import lax
from jax.experimental import pallas as pl
from jax.experimental.pallas import tpu as pltpu
from jax.sharding import PartitionSpec as P

HEADS = 16
HEAD = 72
D = 1152
REACH = 512
ROWS = 768
EXT = ROWS + 2 * REACH
IMAGES = 48
TILE = 256
WINDOW = TILE + 2 * REACH
PARTS = (("xyz", 64, 96), ("yzx", 0, 32), ("xzy", 32, 32))
BLOCK = 160
MAIN = 144
FFB = 256
REM = 13
BIG = -1e30
SCALE = float(HEAD**-0.5 * np.log2(np.e))
NT = (((1,), (1,)), ((), ()))
MESH = pl.DeviceIdType.MESH
F32, BF16 = jnp.float32, jnp.bfloat16


def normalize(values, gain, shift):
    center = values - jnp.mean(values, axis=-1, keepdims=True)
    spread = jnp.mean(center * center, axis=-1, keepdims=True)
    return center * lax.rsqrt(spread + 1e-06) * gain + shift


def gelu(x):
    return 0.5 * x * (1.0 + jnp.tanh(0.7978845608028654 * (x + 0.044715 * (x * x * x))))


def layer_kernel(
    tok, lens, gains, shifts, qkvw_hbm, qkvb, outw_hbm, outb, block, upb, upb_rem, downb,
    out, w,
    halo, qkvw, outw, q_s, k_s, v_s, qx, kx, first, wide, sbuf, mbuf, mixed, acc, hid, hid_r, stage, rest, ru, rd,
    local_sem, stage_sem, halo_send, halo_recv, send, recv, sib_send, sib_recv,
):
    ld, en = lax.axis_index("loader"), lax.axis_index("encoder")
    z, core = ld // 2, ld % 2
    x, y = en // 4, en % 4
    pos = {"x": x, "y": y, "z": z}
    sibling = (z * 2 + 1 - core, en)
    right, left = (ld, (en + 1) % 16), (ld, (en + 15) % 16)

    def device(d, step):
        p = (pos[d] + step) % 4
        if d == "x":
            return (ld, p * 4 + y)
        if d == "y":
            return (ld, x * 4 + p)
        return (p * 2 + core, en)

    qkvw_copy = pltpu.make_async_copy(qkvw_hbm, qkvw, local_sem.at[0])
    outw_copy = pltpu.make_async_copy(outw_hbm, outw, local_sem.at[1])
    own_copy = pltpu.make_async_copy(block, w.at[x, y, :, z, core], local_sem.at[2])
    own_copy.start()
    qkvw_copy.start()
    outw_copy.start()

    barrier = pltpu.get_barrier_semaphore()
    peers = [device(d, s) for d in "xyz" for s in (1, 2, 3)] + [sibling, right, left]
    for peer in peers:
        pl.semaphore_signal(barrier, inc=1, device_id=peer, device_id_type=MESH)
    pl.semaphore_wait(barrier, len(peers))
    own_copy.wait()

    copies = []

    def remote(src, dst, ssem, rsem, to):
        copy = pltpu.make_async_remote_copy(
            src_ref=src, dst_ref=dst, send_sem=ssem, recv_sem=rsem, device_id=to, device_id_type=MESH
        )
        copy.start()
        copies.append(copy)
        return copy

    def region(u, i, phase, at, half):
        order, row, count = PARTS[i]
        index = dict(pos)
        for d in order[:phase]:
            index[d] = pl.ds(0, 4)
        if half is not None:
            index[order[0]] = pl.ds(2 * half, 2)
        index[order[phase]] = at
        return w.at[index["x"], index["y"], u, index["z"], core, pl.ds(row, count)]

    pending = {}

    def move(u, i, phase, at, half, slot, step):
        part = region(u, i, phase, at, half)
        pending[u, i, slot] = remote(
            part, part, send.at[u, i, slot], recv.at[u, i, slot], device(PARTS[i][0][phase], step)
        )

    def to_sibling(u, i, at, half, slot):
        part = region(u, i, 2, at, half)
        pending[u, i, "s", slot] = remote(part, part, sib_send.at[u, i, slot], sib_recv.at[u, i, slot], sibling)

    def phase1(u):
        for i, (order, _, _) in enumerate(PARTS):
            for slot, step in enumerate((1, 3, 2)):
                move(u, i, 0, pos[order[0]], None, slot, step)

    def ring_start(u, phase):
        slot = 3 if phase == 1 else 7
        for i, (order, _, _) in enumerate(PARTS):
            for a in range(3 if phase == 1 else 0):
                pending[u, i, a].wait_recv()
            for s, step in enumerate((1, 3)):
                move(u, i, phase, pos[order[phase]], None, slot + s, step)
            if phase == 2:
                to_sibling(u, i, pos[order[2]], None, 0)

    def ring_forward(u, phase):
        slot = 3 if phase == 1 else 7
        for i, (order, _, _) in enumerate(PARTS):
            for s, step in enumerate((1, 3)):
                pending[u, i, slot + s].wait_recv()
                at = (pos[order[phase]] + 4 - step) % 4
                move(u, i, phase, at, s, slot + 2 + s, step)
                if phase == 2:
                    to_sibling(u, i, at, None, 1 + s)

    def ring_finish(u, phase):
        slot = 3 if phase == 1 else 7
        for i, (order, _, _) in enumerate(PARTS):
            for s in range(2):
                pending[u, i, slot + 2 + s].wait_recv()
                if phase == 2:
                    to_sibling(u, i, (pos[order[2]] + 2) % 4, s, 3 + s)

    def sibling_finish(u):
        for i in range(len(PARTS)):
            for slot in range(5):
                pending[u, i, "s", slot].wait_recv()

    phase1(0)
    halo_copies = {}
    for slot, (row, to) in ((1, (512, right)), (2, (0, left)), (0, (256, right)), (3, (256, left))):
        halo_copies[slot] = remote(
            tok.at[pl.ds(row, 256)], halo.at[slot], halo_send.at[slot], halo_recv.at[slot], to
        )
    phase1(1)

    lengths = lens[...]
    sub = lax.broadcasted_iota(jnp.int32, (IMAGES, IMAGES), 0)
    lan = lax.broadcasted_iota(jnp.int32, (IMAGES, IMAGES), 1)
    ends_column = jnp.sum(jnp.where(lan <= sub, lengths, 0), axis=1, keepdims=True)
    ends = jnp.sum(jnp.where(lan == sub, ends_column, 0), axis=0, keepdims=True)
    base = en * ROWS

    def image_lane(count, offset):
        at = lax.broadcasted_iota(jnp.int32, (count, IMAGES), 0) + (base + offset)
        found = jnp.sum((ends <= at).astype(jnp.int32), axis=1, keepdims=True) + 1
        column = lax.broadcasted_iota(jnp.int32, (count, 1), 0) + (base + offset)
        found = jnp.where(column < 0, 0, found)
        return found + HEAD == lax.broadcasted_iota(jnp.int32, (count, 128), 1)

    def lanes(count):
        return lax.broadcasted_iota(jnp.int32, (count, 128), 1)

    for r in range(0, ROWS, 256):
        qx[r : r + 256] = jnp.where(image_lane(256, r), 0.0, 1.0).astype(BF16)
    for r in range(0, EXT, 256):
        kx[r : r + 256] = jnp.where(image_lane(256, r - REACH), BIG, 0.0).astype(BF16)

    def project(rows_value, row, own):
        first[...] = normalize(rows_value.astype(F32), gains[0:1], shifts[0:1]).astype(BF16)
        for n in range(3):
            cut = slice(n * D, (n + 1) * D)
            product = jnp.dot(first[...], qkvw[:, cut], preferred_element_type=F32) + qkvb[:, cut]
            wide[:, cut] = product.astype(BF16)
        inside = lanes(256) < HEAD
        ones = jnp.where(lanes(256) == HEAD, 1.0, 0.0).astype(BF16)
        for h in range(HEADS):
            for c in range(0 if own else 1, 3):
                lo = h * 3 * HEAD + c * HEAD
                start = lo // 128 * 128
                shift = lo - start
                if shift == 0:
                    piece = wide[:, start : start + 128]
                elif shift + HEAD <= 128:
                    piece = pltpu.roll(wide[:, start : start + 128], 128 - shift, 1)
                else:
                    piece = pltpu.roll(wide[:, start : start + 256], 256 - shift, 1)[:, :128]
                if c == 0:
                    q_s[h, pl.ds(row, 256), :] = jnp.where(inside, piece, qx[pl.ds(row, 256), :])
                elif c == 1:
                    at = row + REACH if own else row
                    k_s[h, pl.ds(at, 256), :] = jnp.where(inside, piece, kx[pl.ds(at, 256), :])
                else:
                    at = row + REACH if own else row
                    v_s[h, pl.ds(at, 256), :] = jnp.where(inside, piece, ones)

    chunk = TILE

    def attention(tile):
        row = tile * TILE

        def scores(h, slot):
            most = None
            for c in range(0, WINDOW, chunk):
                s = lax.dot_general(
                    q_s[h, row : row + TILE, :], k_s[h, row + c : row + c + chunk, :], NT, preferred_element_type=F32
                )
                sbuf[slot, :, c : c + chunk] = s
                for j in range(0, chunk, 128):
                    most = s[:, j : j + 128] if most is None else jnp.maximum(most, s[:, j : j + 128])
            mbuf[slot] = most

        def step(h, now, later):
            peak = jnp.max(mbuf[now], axis=1, keepdims=True) * SCALE
            following = jnp.minimum(h + 1, HEADS - 1)
            total = most = None
            for c in range(0, WINDOW, chunk):
                s = lax.dot_general(
                    q_s[following, row : row + TILE, :],
                    k_s[following, row + c : row + c + chunk, :],
                    NT,
                    preferred_element_type=F32,
                )
                sbuf[later, :, c : c + chunk] = s
                for j in range(0, chunk, 128):
                    most = s[:, j : j + 128] if most is None else jnp.maximum(most, s[:, j : j + 128])
                weights = jnp.exp2(sbuf[now, :, c : c + chunk] * SCALE - peak).astype(BF16)
                part = jnp.dot(weights, v_s[h, row + c : row + c + chunk, :], preferred_element_type=F32)
                total = part if total is None else total + part
            mbuf[later] = most
            q_s[h, row : row + TILE, :] = (total / total[:, HEAD : HEAD + 1]).astype(BF16)

        scores(0, 0)

        def heads(i, carry):
            for j in range(4):
                step(i * 4 + j, j % 2, (j + 1) % 2)
            return carry

        lax.fori_loop(0, HEADS // 4, heads, 0)

    qkvw_copy.wait()
    project(tok[0:256, :], 0, True)
    ring_start(0, 1)
    ring_start(1, 1)
    project(tok[256:512, :], 256, True)
    ring_forward(0, 1)
    ring_forward(1, 1)
    project(tok[512:768, :], 512, True)
    ring_finish(0, 1)
    ring_start(0, 2)

    def inner(i, carry):
        project(halo[1 + i], pl.multiple_of(256 + i * 1024, 256), False)
        return carry

    halo_copies[1].wait_recv()
    halo_copies[2].wait_recv()
    lax.fori_loop(0, 2, inner, 0)
    ring_finish(1, 1)
    attention(1)
    ring_start(1, 2)

    def outer(i, carry):
        project(halo[3 * i], pl.multiple_of(i * 1536, 256), False)
        return carry

    halo_copies[0].wait_recv()
    halo_copies[3].wait_recv()
    lax.fori_loop(0, 2, outer, 0)
    attention(0)
    ring_forward(0, 2)
    attention(2)
    ring_finish(0, 2)
    ring_forward(1, 2)

    outw_copy.wait()
    for h in range(HEADS):
        mixed[:, h * HEAD : (h + 1) * HEAD] = q_s[h, :, 0:HEAD]

    def project_out(i, carry):
        at = pl.ds(pl.multiple_of(i * 256, 256), 256)
        total = tok[at, :].astype(F32) + jnp.dot(mixed[at, :], outw[...], preferred_element_type=F32) + outb[...]
        mixed[at, :] = normalize(total, gains[1:2], shifts[1:2]).astype(BF16)
        acc[at, :] = total + downb[...]
        return carry

    lax.fori_loop(0, 3, project_out, 0)

    def slabs(u, i, slot):
        return pltpu.make_async_copy(
            w.at[i // 2, pl.ds(i % 2 * 2, 2), u, :, :, pl.ds(0, MAIN)], stage.at[slot], stage_sem.at[slot]
        )

    def remainder(u, into):
        copy = pltpu.make_async_copy(w.at[:, :, u, :, :, pl.ds(MAIN, BLOCK - MAIN)], rest, local_sem.at[3])
        copy.start()
        copy.wait()
        for l in range(8):
            piece = rest[:, :, l // 2, l % 2].reshape(256, FFB)
            into[:, l * MAIN : (l + 1) * MAIN] = piece[:, :MAIN]

    def streamed(u, use):
        slabs(u, 0, 0).start()

        def two(i, carry):
            for j in range(2):
                now = 2 * i + j
                slabs(u, now, j).wait()

                @pl.when(now < 7)
                def _():
                    slabs(u, now + 1, 1 - j).start()

                use(now, j)
            return carry

        lax.fori_loop(0, 4, two, 0)

    sibling_finish(0)

    def up(now, slot):
        for j in range(2):
            product = jnp.dot(mixed[...], stage[slot, j].reshape(D, FFB), preferred_element_type=F32)
            hid[2 * now + j] = gelu(product + upb[2 * now + j]).astype(BF16)

    remainder(0, ru)
    streamed(0, up)
    product = lax.dot_general(mixed[...], ru[...], NT, preferred_element_type=F32)
    hid_r[...] = gelu(product + upb_rem[...]).astype(BF16)

    ring_finish(1, 2)
    sibling_finish(1)

    def down(now, slot):
        total = None
        for j in range(2):
            part = lax.dot_general(hid[2 * now + j], stage[slot, j].reshape(D, FFB), NT, preferred_element_type=F32)
            total = part if total is None else total + part
        acc[...] += total

    remainder(1, rd)
    streamed(1, down)
    out[...] = (acc[...] + jnp.dot(hid_r[...], rd[...], preferred_element_type=F32)).astype(BF16)
    for copy in copies:
        copy.wait_send()


def per_device(
    tokens, lengths, norm_gains, norm_shifts, qkv_weight, qkv_bias, out_weight, out_bias, up_weight, up_bias,
    down_weight, down_bias,
):
    wide_pad = ((0, BLOCK - MAIN - REM), (0, FFB - MAIN))
    up_block = jnp.concatenate([up_weight[:, :FFB], jnp.pad(up_weight[:, FFB:].T, wide_pad)], axis=0)
    down_block = jnp.concatenate([down_weight[:FFB].T, jnp.pad(down_weight[FFB:], wide_pad)], axis=0)
    block = jnp.stack([up_block, down_block])
    by_encoder = up_bias.reshape(16, FFB + REM)
    upb = by_encoder[:, None, :FFB]
    upb_rem = jnp.pad(by_encoder[:, FFB:], ((0, 0), (0, 16 - REM))).reshape(1, 256)
    vmem = pl.BlockSpec(memory_space=pltpu.VMEM)
    hbm = pl.BlockSpec(memory_space=pl.ANY)
    dma = pltpu.SemaphoreType.DMA
    out, _ = pl.pallas_call(
        layer_kernel,
        out_shape=[
            jax.ShapeDtypeStruct((ROWS, D), BF16),
            jax.ShapeDtypeStruct((4, 4, 2, 4, 2, BLOCK, FFB), BF16),
        ],
        in_specs=[vmem, vmem, vmem, vmem, hbm, vmem, hbm, vmem, vmem, vmem, vmem, vmem],
        out_specs=[vmem, hbm],
        scratch_shapes=[
            pltpu.VMEM((4, 256, D), BF16),
            pltpu.VMEM((D, 3 * D), BF16),
            pltpu.VMEM((D, D), BF16),
            pltpu.VMEM((HEADS, ROWS, 128), BF16),
            pltpu.VMEM((HEADS, EXT, 128), BF16),
            pltpu.VMEM((HEADS, EXT, 128), BF16),
            pltpu.VMEM((ROWS, 128), BF16),
            pltpu.VMEM((EXT, 128), BF16),
            pltpu.VMEM((256, D), BF16),
            pltpu.VMEM((256, 3 * D), BF16),
            pltpu.VMEM((2, TILE, WINDOW), F32),
            pltpu.VMEM((2, TILE, 128), F32),
            pltpu.VMEM((ROWS, D), BF16),
            pltpu.VMEM((ROWS, D), F32),
            pltpu.VMEM((16, ROWS, FFB), BF16),
            pltpu.VMEM((ROWS, 256), BF16),
            pltpu.VMEM((2, 2, 4, 2, MAIN, FFB), BF16),
            pltpu.VMEM((4, 4, 4, 2, BLOCK - MAIN, FFB), BF16),
            pltpu.VMEM((256, D), BF16),
            pltpu.VMEM((256, D), BF16),
            dma((4,)),
            dma((2,)),
            dma((4,)),
            dma((4,)),
            dma((2, 3, 11)),
            dma((2, 3, 11)),
            dma((2, 3, 5)),
            dma((2, 3, 5)),
        ],
        compiler_params=pltpu.CompilerParams(
            collective_id=0, has_side_effects=True, vmem_limit_bytes=62 * 2**20
        ),
        cost_estimate=pl.CostEstimate(flops=40_000_000_000, bytes_accessed=50_000_000, transcendentals=20_000_000),
    )(
        tokens, lengths, norm_gains, norm_shifts, qkv_weight, qkv_bias[None], out_weight, out_bias[None], block,
        upb, upb_rem, down_bias[None],
    )
    return out


def solution(mesh):
    placed = (
        P(("loader", "encoder"), None),
        P("loader", None),
        P(),
        P(),
        P(),
        P(),
        P(),
        P(),
        P("loader", "encoder"),
        P(),
        P("encoder", "loader"),
        P(),
    )
    return jax.shard_map(
        per_device,
        mesh=mesh,
        in_specs=placed,
        out_specs=P(("loader", "encoder"), None),
        check_vma=False,
    )
```

```python
import functools

import jax
import jax.numpy as jnp
import numpy as np
from jax import lax
from jax.experimental import pallas as pl
from jax.experimental.pallas import tpu as pltpu
from jax.sharding import PartitionSpec as P

HEADS = 16
HEAD = 72
D = 1152
REACH = 512
ROWS = 768
EXT = ROWS + 2 * REACH
IMAGES = 48
TILE = 256
WINDOW = TILE + 2 * REACH
PARTS = (("xyz", 96, 64), ("yzx", 0, 48), ("zxy", 48, 48))
BLOCK = 160
MAIN = 144
FFB = 256
REM = 13
BIG = -1e30
SCALE = float(HEAD**-0.5 * np.log2(np.e))
NT = (((1,), (1,)), ((), ()))
MESH = pl.DeviceIdType.MESH
F32, BF16 = jnp.float32, jnp.bfloat16


def normalize(values, gain, shift):
    center = values - jnp.mean(values, axis=-1, keepdims=True)
    spread = jnp.mean(center * center, axis=-1, keepdims=True)
    return center * lax.rsqrt(spread + 1e-06) * gain + shift


def gelu(x):
    return 0.5 * x * (1.0 + jnp.tanh(0.7978845608028654 * (x + 0.044715 * (x * x * x))))


def layer_kernel(
    tok, lens, gains, shifts, qkvw_hbm, qkv_bias, outw_hbm, out_bias, up_own, up_bias, down_own, down_bias,
    out, w,
    block, turned, qkvb, outb, downb, upb, upb_rem, halo, qkvw, outw, q_s, k_s, v_s, qx, kx, first, wide, sbuf, mbuf, mixed, acc, hid, hid_r, stage, rest, ru, rd,
    local_sem, stage_sem, halo_send, halo_recv, send, recv, sib_send, sib_recv,
):
    ld, en = lax.axis_index("loader"), lax.axis_index("encoder")
    z, core = ld // 2, ld % 2
    x, y = en // 4, en % 4
    pos = {"x": x, "y": y, "z": z}
    sibling = (z * 2 + 1 - core, en)
    right, left = (ld, (en + 1) % 16), (ld, (en + 15) % 16)

    def device(d, step):
        p = (pos[d] + step) % 4
        if d == "x":
            return (ld, p * 4 + y)
        if d == "y":
            return (ld, x * 4 + p)
        return (p * 2 + core, en)

    qkvw_copy = pltpu.make_async_copy(qkvw_hbm, qkvw, local_sem.at[0])
    outw_copy = pltpu.make_async_copy(outw_hbm, outw, local_sem.at[1])
    own_copy = pltpu.make_async_copy(block, w.at[x, y, :, z, core], local_sem.at[2])
    qkvw_copy.start()

    barrier = pltpu.get_barrier_semaphore()
    peers = [device(d, s) for d in "xyz" for s in (1, 2, 3)] + [sibling, right, left]
    for peer in peers:
        pl.semaphore_signal(barrier, inc=1, device_id=peer, device_id_type=MESH)

    block[...] = jnp.zeros_like(block)
    turned[...] = jnp.zeros_like(turned)
    block[0, 0:MAIN, :] = up_own[:, 0:FFB]
    turned[0:MAIN, 0:REM] = up_own[:, FFB : FFB + REM].astype(F32)
    block[0, MAIN:BLOCK, :] = jnp.transpose(turned[:, 0:128])[0:16].astype(BF16)
    turned[:, 0:MAIN] = down_own[0:FFB, :].astype(F32)
    block[1, 0:MAIN, :] = jnp.transpose(turned[...])[0:MAIN].astype(BF16)
    turned[0:REM, 0:MAIN] = down_own[FFB : FFB + REM, :].astype(F32)
    turned[REM:16, :] = jnp.zeros((16 - REM, FFB), F32)
    block[1, MAIN:BLOCK, 0:MAIN] = turned[0:16, 0:MAIN].astype(BF16)
    own_copy.start()
    pl.semaphore_wait(barrier, len(peers))
    own_copy.wait()
    outw_copy.start()

    copies = []

    def remote(src, dst, ssem, rsem, to):
        copy = pltpu.make_async_remote_copy(
            src_ref=src, dst_ref=dst, send_sem=ssem, recv_sem=rsem, device_id=to, device_id_type=MESH
        )
        copy.start()
        copies.append(copy)
        return copy

    def region(u, i, phase, at, half):
        order, row, count = PARTS[i]
        index = dict(pos)
        for d in order[:phase]:
            index[d] = pl.ds(0, 4)
        if half is not None:
            index[order[0]] = pl.ds(2 * half, 2)
        index[order[phase]] = at
        return w.at[index["x"], index["y"], u, index["z"], core, pl.ds(row, count)]

    pending = {}

    def move(u, i, phase, at, half, slot, step):
        part = region(u, i, phase, at, half)
        pending[u, i, slot] = remote(
            part, part, send.at[u, i, slot], recv.at[u, i, slot], device(PARTS[i][0][phase], step)
        )

    def to_sibling(u, i, at, half, slot):
        part = region(u, i, 2, at, half)
        pending[u, i, "s", slot] = remote(part, part, sib_send.at[u, i, slot], sib_recv.at[u, i, slot], sibling)

    def phase1(u):
        for i, (order, _, _) in enumerate(PARTS):
            for slot, step in enumerate((1, 3, 2)):
                move(u, i, 0, pos[order[0]], None, slot, step)

    def ring_start(u, phase):
        slot = 3 if phase == 1 else 7
        for i, (order, _, _) in enumerate(PARTS):
            for a in range(3 if phase == 1 else 0):
                pending[u, i, a].wait_recv()
            for s, step in enumerate((1, 3)):
                move(u, i, phase, pos[order[phase]], None, slot + s, step)
            if phase == 2:
                to_sibling(u, i, pos[order[2]], None, 0)

    def ring_forward(u, phase):
        slot = 3 if phase == 1 else 7
        for i, (order, _, _) in enumerate(PARTS):
            for s, step in enumerate((1, 3)):
                pending[u, i, slot + s].wait_recv()
                at = (pos[order[phase]] + 4 - step) % 4
                move(u, i, phase, at, s, slot + 2 + s, step)
                if phase == 2:
                    to_sibling(u, i, at, None, 1 + s)

    def ring_finish(u, phase):
        slot = 3 if phase == 1 else 7
        for i, (order, _, _) in enumerate(PARTS):
            for s in range(2):
                pending[u, i, slot + 2 + s].wait_recv()
                if phase == 2:
                    to_sibling(u, i, (pos[order[2]] + 2) % 4, s, 3 + s)

    def sibling_finish(u):
        for i in range(len(PARTS)):
            for slot in range(5):
                pending[u, i, "s", slot].wait_recv()

    phase1(0)
    halo_copies = {}
    for slot, (row, to) in ((1, (512, right)), (2, (0, left))):
        halo_copies[slot] = remote(
            tok.at[pl.ds(row, 256)], halo.at[slot], halo_send.at[slot], halo_recv.at[slot], to
        )
    phase1(1)
    middle = tok.at[pl.ds(256, 256)]

    def outer_copy(slot, to):
        return pltpu.make_async_remote_copy(
            src_ref=middle, dst_ref=halo.at[slot], send_sem=halo_send.at[slot], recv_sem=halo_recv.at[slot],
            device_id=to, device_id_type=MESH,
        )

    def outer_start():
        outer_copy(0, right).start()
        outer_copy(3, left).start()

    def outer_sent():
        for slot in (0, 3):
            outer_copy(slot, right).wait_send()

    lengths = lens[...]
    sub = lax.broadcasted_iota(jnp.int32, (IMAGES, IMAGES), 0)
    lan = lax.broadcasted_iota(jnp.int32, (IMAGES, IMAGES), 1)
    ends_column = jnp.sum(jnp.where(lan <= sub, lengths, 0), axis=1, keepdims=True)
    ends = jnp.sum(jnp.where(lan == sub, ends_column, 0), axis=0, keepdims=True)
    base = en * ROWS

    def image_lane(count, offset):
        at = lax.broadcasted_iota(jnp.int32, (count, IMAGES), 0) + (base + offset)
        found = jnp.sum((ends <= at).astype(jnp.int32), axis=1, keepdims=True) + 1
        column = lax.broadcasted_iota(jnp.int32, (count, 1), 0) + (base + offset)
        found = jnp.where(column < 0, 0, found)
        return found + HEAD == lax.broadcasted_iota(jnp.int32, (count, 128), 1)

    def lanes(count):
        return lax.broadcasted_iota(jnp.int32, (count, 128), 1)

    qkvb[...] = qkv_bias[...].reshape(1, 3 * D)
    outb[...] = out_bias[...].reshape(1, D)
    downb[...] = down_bias[...].reshape(1, D)
    upb_row = up_bias[...].reshape(1, 16 * (FFB + REM))
    upb_rem[...] = jnp.zeros_like(upb_rem)
    for e in range(16):
        lo = e * (FFB + REM)
        upb[e] = upb_row[:, lo : lo + FFB]
        upb_rem[:, e * 16 : e * 16 + REM] = upb_row[:, lo + FFB : lo + FFB + REM]
    for r in range(0, ROWS, 256):
        qx[r : r + 256] = jnp.where(image_lane(256, r), 0.0, 1.0).astype(BF16)
    for r in range(0, EXT, 256):
        kx[r : r + 256] = jnp.where(image_lane(256, r - REACH), BIG, 0.0).astype(BF16)

    def project(rows_value, row, own):
        first[...] = normalize(rows_value.astype(F32), gains[0:1], shifts[0:1]).astype(BF16)
        for n in range(3):
            cut = slice(n * D, (n + 1) * D)
            product = jnp.dot(first[...], qkvw[:, cut], preferred_element_type=F32) + qkvb[:, cut]
            wide[:, cut] = product.astype(BF16)
        inside = lanes(256) < HEAD
        ones = jnp.where(lanes(256) == HEAD, 1.0, 0.0).astype(BF16)
        for h in range(HEADS):
            for c in range(0 if own else 1, 3):
                lo = h * 3 * HEAD + c * HEAD
                start = lo // 128 * 128
                shift = lo - start
                if shift == 0:
                    piece = wide[:, start : start + 128]
                elif shift + HEAD <= 128:
                    piece = pltpu.roll(wide[:, start : start + 128], 128 - shift, 1)
                else:
                    piece = pltpu.roll(wide[:, start : start + 256], 256 - shift, 1)[:, :128]
                if c == 0:
                    q_s[h, pl.ds(row, 256), :] = jnp.where(inside, piece, qx[pl.ds(row, 256), :])
                elif c == 1:
                    at = row + REACH if own else row
                    k_s[h, pl.ds(at, 256), :] = jnp.where(inside, piece, kx[pl.ds(at, 256), :])
                else:
                    at = row + REACH if own else row
                    v_s[h, pl.ds(at, 256), :] = jnp.where(inside, piece, ones)

    chunk = TILE

    def attention(tile):
        row = tile * TILE

        def scores(h, slot):
            most = None
            for c in range(0, WINDOW, chunk):
                s = lax.dot_general(
                    q_s[h, row : row + TILE, :], k_s[h, row + c : row + c + chunk, :], NT, preferred_element_type=F32
                )
                sbuf[slot, :, c : c + chunk] = s
                for j in range(0, chunk, 128):
                    most = s[:, j : j + 128] if most is None else jnp.maximum(most, s[:, j : j + 128])
            mbuf[slot] = most

        def step(h, now, later):
            peak = jnp.max(mbuf[now], axis=1, keepdims=True) * SCALE
            following = jnp.minimum(h + 1, HEADS - 1)
            total = most = None
            for c in range(0, WINDOW, chunk):
                s = lax.dot_general(
                    q_s[following, row : row + TILE, :],
                    k_s[following, row + c : row + c + chunk, :],
                    NT,
                    preferred_element_type=F32,
                )
                sbuf[later, :, c : c + chunk] = s
                for j in range(0, chunk, 128):
                    most = s[:, j : j + 128] if most is None else jnp.maximum(most, s[:, j : j + 128])
                weights = jnp.exp2(sbuf[now, :, c : c + chunk] * SCALE - peak).astype(BF16)
                part = jnp.dot(weights, v_s[h, row + c : row + c + chunk, :], preferred_element_type=F32)
                total = part if total is None else total + part
            mbuf[later] = most
            q_s[h, row : row + TILE, :] = (total / total[:, HEAD : HEAD + 1]).astype(BF16)

        scores(0, 0)

        def heads(i, carry):
            for j in range(4):
                step(i * 4 + j, j % 2, (j + 1) % 2)
            return carry

        lax.fori_loop(0, HEADS // 4, heads, 0)

    qkvw_copy.wait()
    project(tok[0:256, :], 0, True)
    ring_start(0, 1)
    ring_start(1, 1)
    project(tok[256:512, :], 256, True)
    project(tok[512:768, :], 512, True)
    ring_forward(0, 1)
    ring_forward(1, 1)
    outer_start()

    def inner(i, carry):
        project(halo[1 + i], pl.multiple_of(256 + i * 1024, 256), False)
        return carry

    halo_copies[1].wait_recv()
    halo_copies[2].wait_recv()
    lax.fori_loop(0, 2, inner, 0)
    ring_finish(0, 1)
    ring_start(0, 2)
    ring_finish(1, 1)
    ring_start(1, 2)
    attention(1)
    ring_forward(0, 2)

    def outer(i, carry):
        project(halo[3 * i], pl.multiple_of(i * 1536, 256), False)
        return carry

    for slot in (0, 3):
        outer_copy(slot, right).wait_recv()
    lax.fori_loop(0, 2, outer, 0)
    attention(0)
    ring_finish(0, 2)
    ring_forward(1, 2)
    attention(2)

    outw_copy.wait()
    for h in range(HEADS):
        mixed[:, h * HEAD : (h + 1) * HEAD] = q_s[h, :, 0:HEAD]

    def project_out(i, carry):
        at = pl.ds(pl.multiple_of(i * 256, 256), 256)
        total = tok[at, :].astype(F32) + jnp.dot(mixed[at, :], outw[...], preferred_element_type=F32) + outb[...]
        mixed[at, :] = normalize(total, gains[1:2], shifts[1:2]).astype(BF16)
        acc[at, :] = total + downb[...]
        return carry

    lax.fori_loop(0, 3, project_out, 0)
    ring_finish(1, 2)

    def slabs(u, i, slot):
        return pltpu.make_async_copy(
            w.at[i // 2, pl.ds(i % 2 * 2, 2), u, :, :, pl.ds(0, MAIN)], stage.at[slot], stage_sem.at[slot]
        )

    def remainder(u, into):
        copy = pltpu.make_async_copy(w.at[:, :, u, :, :, pl.ds(MAIN, BLOCK - MAIN)], rest, local_sem.at[3])
        copy.start()
        copy.wait()
        for l in range(8):
            piece = rest[:, :, l // 2, l % 2].reshape(256, FFB)
            into[:, l * MAIN : (l + 1) * MAIN] = piece[:, :MAIN]

    def streamed(u, use):
        slabs(u, 0, 0).start()

        def two(i, carry):
            for j in range(2):
                now = 2 * i + j
                slabs(u, now, j).wait()

                @pl.when(now < 7)
                def _():
                    slabs(u, now + 1, 1 - j).start()

                use(now, j)
            return carry

        lax.fori_loop(0, 4, two, 0)

    sibling_finish(0)

    def up(now, slot):
        for j in range(2):
            product = jnp.dot(mixed[...], stage[slot, j].reshape(D, FFB), preferred_element_type=F32)
            hid[2 * now + j] = gelu(product + upb[2 * now + j]).astype(BF16)

    remainder(0, ru)
    streamed(0, up)
    product = lax.dot_general(mixed[...], ru[...], NT, preferred_element_type=F32)
    hid_r[...] = gelu(product + upb_rem[...]).astype(BF16)

    sibling_finish(1)

    def down(now, slot):
        total = None
        for j in range(2):
            part = lax.dot_general(hid[2 * now + j], stage[slot, j].reshape(D, FFB), NT, preferred_element_type=F32)
            total = part if total is None else total + part
        acc[...] += total

    remainder(1, rd)
    streamed(1, down)
    out[...] = (acc[...] + jnp.dot(hid_r[...], rd[...], preferred_element_type=F32)).astype(BF16)
    outer_sent()
    for copy in copies:
        copy.wait_send()


def per_device(
    tokens, lengths, norm_gains, norm_shifts, qkv_weight, qkv_bias, out_weight, out_bias, up_weight, up_bias,
    down_weight, down_bias,
):
    vmem = pl.BlockSpec(memory_space=pltpu.VMEM)
    hbm = pl.BlockSpec(memory_space=pl.ANY)
    dma = pltpu.SemaphoreType.DMA
    out, _ = pl.pallas_call(
        layer_kernel,
        out_shape=[
            jax.ShapeDtypeStruct((ROWS, D), BF16),
            jax.ShapeDtypeStruct((4, 4, 2, 4, 2, BLOCK, FFB), BF16),
        ],
        in_specs=[vmem, vmem, vmem, vmem, hbm, vmem, hbm, vmem, vmem, vmem, vmem, vmem],
        out_specs=[vmem, hbm],
        scratch_shapes=[
            pltpu.VMEM((2, BLOCK, FFB), BF16),
            pltpu.VMEM((FFB, FFB), F32),
            pltpu.VMEM((1, 3 * D), F32),
            pltpu.VMEM((1, D), F32),
            pltpu.VMEM((1, D), F32),
            pltpu.VMEM((16, 1, FFB), F32),
            pltpu.VMEM((1, 256), F32),
            pltpu.VMEM((4, 256, D), BF16),
            pltpu.VMEM((D, 3 * D), BF16),
            pltpu.VMEM((D, D), BF16),
            pltpu.VMEM((HEADS, ROWS, 128), BF16),
            pltpu.VMEM((HEADS, EXT, 128), BF16),
            pltpu.VMEM((HEADS, EXT, 128), BF16),
            pltpu.VMEM((ROWS, 128), BF16),
            pltpu.VMEM((EXT, 128), BF16),
            pltpu.VMEM((256, D), BF16),
            pltpu.VMEM((256, 3 * D), BF16),
            pltpu.VMEM((2, TILE, WINDOW), F32),
            pltpu.VMEM((2, TILE, 128), F32),
            pltpu.VMEM((ROWS, D), BF16),
            pltpu.VMEM((ROWS, D), F32),
            pltpu.VMEM((16, ROWS, FFB), BF16),
            pltpu.VMEM((ROWS, 256), BF16),
            pltpu.VMEM((2, 2, 4, 2, MAIN, FFB), BF16),
            pltpu.VMEM((4, 4, 4, 2, BLOCK - MAIN, FFB), BF16),
            pltpu.VMEM((256, D), BF16),
            pltpu.VMEM((256, D), BF16),
            dma((4,)),
            dma((2,)),
            dma((4,)),
            dma((4,)),
            dma((2, 3, 11)),
            dma((2, 3, 11)),
            dma((2, 3, 5)),
            dma((2, 3, 5)),
        ],
        compiler_params=pltpu.CompilerParams(
            collective_id=0, has_side_effects=True, vmem_limit_bytes=62 * 2**20
        ),
        cost_estimate=pl.CostEstimate(flops=40_000_000_000, bytes_accessed=50_000_000, transcendentals=20_000_000),
    )(
        tokens, lengths, norm_gains, norm_shifts, qkv_weight, qkv_bias, out_weight, out_bias, up_weight, up_bias,
        down_weight, down_bias,
    )
    return out


def solution(mesh):
    placed = (
        P(("loader", "encoder"), None),
        P("loader", None),
        P(),
        P(),
        P(),
        P(),
        P(),
        P(),
        P("loader", "encoder"),
        P(),
        P("encoder", "loader"),
        P(),
    )
    return jax.shard_map(
        per_device,
        mesh=mesh,
        in_specs=placed,
        out_specs=P(("loader", "encoder"), None),
        check_vma=False,
    )
```

```python
import functools

import jax
import jax.numpy as jnp
import numpy as np
from jax import lax
from jax.experimental import pallas as pl
from jax.experimental.pallas import tpu as pltpu
from jax.sharding import PartitionSpec as P

HEADS = 16
HEAD = 72
D = 1152
REACH = 512
ROWS = 768
EXT = ROWS + 2 * REACH
IMAGES = 48
TILE = 256
WINDOW = TILE + 2 * REACH
PARTS = (("xyz", 96, 64), ("yzx", 0, 48), ("zxy", 48, 48))
BLOCK = 160
MAIN = 144
FFB = 256
REM = 13
BIG = -1e30
SCALE = float(HEAD**-0.5 * np.log2(np.e))
NT = (((1,), (1,)), ((), ()))
MESH = pl.DeviceIdType.MESH
F32, BF16 = jnp.float32, jnp.bfloat16


def normalize(values, gain, shift):
    center = values - jnp.mean(values, axis=-1, keepdims=True)
    spread = jnp.mean(center * center, axis=-1, keepdims=True)
    return center * lax.rsqrt(spread + 1e-06) * gain + shift


def gelu(x):
    return 0.5 * x * (1.0 + jnp.tanh(0.7978845608028654 * (x + 0.044715 * (x * x * x))))


def layer_kernel(
    tok, lens, gains, shifts, qkvw_hbm, qkv_bias, outw_hbm, out_bias, up_own, up_bias, down_own, down_bias,
    out, w,
    block, turned, qkvb, outb, downb, upb, upb_rem, halo, qkvw, outw, q_s, k_s, v_s, qx, kx, first, wide, sbuf, mbuf, mixed, acc, hid, hid_r, stage, rest, ru, rd,
    local_sem, stage_sem, halo_send, halo_recv, send, recv, sib_send, sib_recv,
):
    ld, en = lax.axis_index("loader"), lax.axis_index("encoder")
    z, core = ld // 2, ld % 2
    x, y = en // 4, en % 4
    pos = {"x": x, "y": y, "z": z}
    sibling = (z * 2 + 1 - core, en)
    right, left = (ld, (en + 1) % 16), (ld, (en + 15) % 16)

    def device(d, step):
        p = (pos[d] + step) % 4
        if d == "x":
            return (ld, p * 4 + y)
        if d == "y":
            return (ld, x * 4 + p)
        return (p * 2 + core, en)

    qkvw_copy = pltpu.make_async_copy(qkvw_hbm, qkvw, local_sem.at[0])
    outw_copy = pltpu.make_async_copy(outw_hbm, outw, local_sem.at[1])
    own_copy = pltpu.make_async_copy(block, w.at[x, y, :, z, core], local_sem.at[2])
    qkvw_copy.start()

    barrier = pltpu.get_barrier_semaphore()
    peers = [device(d, s) for d in "xyz" for s in (1, 2, 3)] + [sibling, right, left]
    for peer in peers:
        pl.semaphore_signal(barrier, inc=1, device_id=peer, device_id_type=MESH)

    block[...] = jnp.zeros_like(block)
    turned[...] = jnp.zeros_like(turned)
    block[0, 0:MAIN, :] = up_own[:, 0:FFB]
    turned[0:MAIN, 0:REM] = up_own[:, FFB : FFB + REM].astype(F32)
    block[0, MAIN:BLOCK, :] = jnp.transpose(turned[:, 0:128])[0:16].astype(BF16)
    turned[:, 0:MAIN] = down_own[0:FFB, :].astype(F32)
    block[1, 0:MAIN, :] = jnp.transpose(turned[...])[0:MAIN].astype(BF16)
    turned[0:REM, 0:MAIN] = down_own[FFB : FFB + REM, :].astype(F32)
    turned[REM:16, :] = jnp.zeros((16 - REM, FFB), F32)
    block[1, MAIN:BLOCK, 0:MAIN] = turned[0:16, 0:MAIN].astype(BF16)
    own_copy.start()
    pl.semaphore_wait(barrier, len(peers))
    own_copy.wait()
    outw_copy.start()

    copies = []

    def remote(src, dst, ssem, rsem, to):
        copy = pltpu.make_async_remote_copy(
            src_ref=src, dst_ref=dst, send_sem=ssem, recv_sem=rsem, device_id=to, device_id_type=MESH
        )
        copy.start()
        copies.append(copy)
        return copy

    def region(u, i, phase, at, half):
        order, row, count = PARTS[i]
        index = dict(pos)
        for d in order[:phase]:
            index[d] = pl.ds(0, 4)
        if half is not None:
            index[order[0]] = pl.ds(2 * half, 2)
        index[order[phase]] = at
        return w.at[index["x"], index["y"], u, index["z"], core, pl.ds(row, count)]

    pending = {}

    def move(u, i, phase, at, half, slot, step):
        part = region(u, i, phase, at, half)
        pending[u, i, slot] = remote(
            part, part, send.at[u, i, slot], recv.at[u, i, slot], device(PARTS[i][0][phase], step)
        )

    def to_sibling(u, i, at, half, slot):
        part = region(u, i, 2, at, half)
        pending[u, i, "s", slot] = remote(part, part, sib_send.at[u, i, slot], sib_recv.at[u, i, slot], sibling)

    def phase1(u):
        for i, (order, _, _) in enumerate(PARTS):
            for slot, step in enumerate((1, 3, 2)):
                move(u, i, 0, pos[order[0]], None, slot, step)

    def ring_start(u, phase):
        slot = 3 if phase == 1 else 7
        for i, (order, _, _) in enumerate(PARTS):
            for a in range(3 if phase == 1 else 0):
                pending[u, i, a].wait_recv()
            for s, step in enumerate((1, 3)):
                move(u, i, phase, pos[order[phase]], None, slot + s, step)
            if phase == 2:
                to_sibling(u, i, pos[order[2]], None, 0)

    def ring_forward(u, phase):
        slot = 3 if phase == 1 else 7
        for i, (order, _, _) in enumerate(PARTS):
            for s, step in enumerate((1, 3)):
                pending[u, i, slot + s].wait_recv()
                at = (pos[order[phase]] + 4 - step) % 4
                move(u, i, phase, at, s, slot + 2 + s, step)
                if phase == 2:
                    to_sibling(u, i, at, None, 1 + s)

    def ring_finish(u, phase):
        slot = 3 if phase == 1 else 7
        for i, (order, _, _) in enumerate(PARTS):
            for s in range(2):
                pending[u, i, slot + 2 + s].wait_recv()
                if phase == 2:
                    to_sibling(u, i, (pos[order[2]] + 2) % 4, s, 3 + s)

    def sibling_finish(u):
        for i in range(len(PARTS)):
            for slot in range(5):
                pending[u, i, "s", slot].wait_recv()

    phase1(0)
    phase1(1)
    halo_copies = {}
    for slot, (row, to) in ((1, (512, right)), (2, (0, left))):
        halo_copies[slot] = remote(
            tok.at[pl.ds(row, 256)], halo.at[slot], halo_send.at[slot], halo_recv.at[slot], to
        )
    middle = tok.at[pl.ds(256, 256)]

    def outer_copy(slot, to):
        return pltpu.make_async_remote_copy(
            src_ref=middle, dst_ref=halo.at[slot], send_sem=halo_send.at[slot], recv_sem=halo_recv.at[slot],
            device_id=to, device_id_type=MESH,
        )

    def outer_start():
        outer_copy(0, right).start()
        outer_copy(3, left).start()

    def outer_sent():
        for slot in (0, 3):
            outer_copy(slot, right).wait_send()

    lengths = lens[...]
    sub = lax.broadcasted_iota(jnp.int32, (IMAGES, IMAGES), 0)
    lan = lax.broadcasted_iota(jnp.int32, (IMAGES, IMAGES), 1)
    ends_column = jnp.sum(jnp.where(lan <= sub, lengths, 0), axis=1, keepdims=True)
    ends = jnp.sum(jnp.where(lan == sub, ends_column, 0), axis=0, keepdims=True)
    base = en * ROWS

    def image_lane(count, offset):
        at = lax.broadcasted_iota(jnp.int32, (count, IMAGES), 0) + (base + offset)
        found = jnp.sum((ends <= at).astype(jnp.int32), axis=1, keepdims=True) + 1
        column = lax.broadcasted_iota(jnp.int32, (count, 1), 0) + (base + offset)
        found = jnp.where(column < 0, 0, found)
        return found + HEAD == lax.broadcasted_iota(jnp.int32, (count, 128), 1)

    def lanes(count):
        return lax.broadcasted_iota(jnp.int32, (count, 128), 1)

    qkvb[...] = qkv_bias[...].reshape(1, 3 * D)
    outb[...] = out_bias[...].reshape(1, D)
    downb[...] = down_bias[...].reshape(1, D)
    upb_row = up_bias[...].reshape(1, 16 * (FFB + REM))
    upb_rem[...] = jnp.zeros_like(upb_rem)
    for e in range(16):
        lo = e * (FFB + REM)
        upb[e] = upb_row[:, lo : lo + FFB]
        upb_rem[:, e * 16 : e * 16 + REM] = upb_row[:, lo + FFB : lo + FFB + REM]
    for r in range(0, ROWS, 256):
        qx[r : r + 256] = jnp.where(image_lane(256, r), 0.0, 1.0).astype(BF16)
    for r in range(0, EXT, 256):
        kx[r : r + 256] = jnp.where(image_lane(256, r - REACH), BIG, 0.0).astype(BF16)

    def project(rows_value, row, own):
        first[...] = normalize(rows_value.astype(F32), gains[0:1], shifts[0:1]).astype(BF16)
        for n in range(3):
            cut = slice(n * D, (n + 1) * D)
            product = jnp.dot(first[...], qkvw[:, cut], preferred_element_type=F32) + qkvb[:, cut]
            wide[:, cut] = product.astype(BF16)
        inside = lanes(256) < HEAD
        ones = jnp.where(lanes(256) == HEAD, 1.0, 0.0).astype(BF16)
        for h in range(HEADS):
            for c in range(0 if own else 1, 3):
                lo = h * 3 * HEAD + c * HEAD
                start = lo // 128 * 128
                shift = lo - start
                if shift == 0:
                    piece = wide[:, start : start + 128]
                elif shift + HEAD <= 128:
                    piece = pltpu.roll(wide[:, start : start + 128], 128 - shift, 1)
                else:
                    piece = pltpu.roll(wide[:, start : start + 256], 256 - shift, 1)[:, :128]
                if c == 0:
                    q_s[h, pl.ds(row, 256), :] = jnp.where(inside, piece, qx[pl.ds(row, 256), :])
                elif c == 1:
                    at = row + REACH if own else row
                    k_s[h, pl.ds(at, 256), :] = jnp.where(inside, piece, kx[pl.ds(at, 256), :])
                else:
                    at = row + REACH if own else row
                    v_s[h, pl.ds(at, 256), :] = jnp.where(inside, piece, ones)

    chunk = TILE

    def attention(tile):
        row = tile * TILE

        def scores(h, slot):
            most = None
            for c in range(0, WINDOW, chunk):
                s = lax.dot_general(
                    q_s[h, row : row + TILE, :], k_s[h, row + c : row + c + chunk, :], NT, preferred_element_type=F32
                )
                sbuf[slot, :, c : c + chunk] = s
                for j in range(0, chunk, 128):
                    most = s[:, j : j + 128] if most is None else jnp.maximum(most, s[:, j : j + 128])
            mbuf[slot] = most

        def step(h, now, later):
            peak = jnp.max(mbuf[now], axis=1, keepdims=True) * SCALE
            following = jnp.minimum(h + 1, HEADS - 1)
            total = most = None
            for c in range(0, WINDOW, chunk):
                s = lax.dot_general(
                    q_s[following, row : row + TILE, :],
                    k_s[following, row + c : row + c + chunk, :],
                    NT,
                    preferred_element_type=F32,
                )
                sbuf[later, :, c : c + chunk] = s
                for j in range(0, chunk, 128):
                    most = s[:, j : j + 128] if most is None else jnp.maximum(most, s[:, j : j + 128])
                weights = jnp.exp2(sbuf[now, :, c : c + chunk] * SCALE - peak).astype(BF16)
                part = jnp.dot(weights, v_s[h, row + c : row + c + chunk, :], preferred_element_type=F32)
                total = part if total is None else total + part
            mbuf[later] = most
            q_s[h, row : row + TILE, :] = (total / total[:, HEAD : HEAD + 1]).astype(BF16)

        scores(0, 0)

        def heads(i, carry):
            for j in range(4):
                step(i * 4 + j, j % 2, (j + 1) % 2)
            return carry

        lax.fori_loop(0, HEADS // 4, heads, 0)

    qkvw_copy.wait()
    project(tok[0:256, :], 0, True)
    ring_start(0, 1)
    ring_start(1, 1)
    project(tok[256:512, :], 256, True)
    project(tok[512:768, :], 512, True)
    ring_forward(0, 1)
    ring_forward(1, 1)
    outer_start()

    def inner(i, carry):
        project(halo[1 + i], pl.multiple_of(256 + i * 1024, 256), False)
        return carry

    halo_copies[1].wait_recv()
    halo_copies[2].wait_recv()
    lax.fori_loop(0, 2, inner, 0)
    ring_finish(0, 1)
    ring_start(0, 2)
    ring_finish(1, 1)
    ring_start(1, 2)
    attention(1)

    def outer(i, carry):
        project(halo[3 * i], pl.multiple_of(i * 1536, 256), False)
        return carry

    for slot in (0, 3):
        outer_copy(slot, right).wait_recv()
    lax.fori_loop(0, 2, outer, 0)
    ring_forward(0, 2)
    attention(0)
    ring_finish(0, 2)
    ring_forward(1, 2)
    attention(2)

    outw_copy.wait()
    for h in range(HEADS):
        mixed[:, h * HEAD : (h + 1) * HEAD] = q_s[h, :, 0:HEAD]

    def project_out(i, carry):
        at = pl.ds(pl.multiple_of(i * 256, 256), 256)
        total = tok[at, :].astype(F32) + jnp.dot(mixed[at, :], outw[...], preferred_element_type=F32) + outb[...]
        mixed[at, :] = normalize(total, gains[1:2], shifts[1:2]).astype(BF16)
        acc[at, :] = total + downb[...]
        return carry

    lax.fori_loop(0, 3, project_out, 0)
    ring_finish(1, 2)

    def slabs(u, i, slot):
        return pltpu.make_async_copy(
            w.at[i // 2, pl.ds(i % 2 * 2, 2), u, :, :, pl.ds(0, MAIN)], stage.at[slot], stage_sem.at[slot]
        )

    def remainder(u, into):
        copy = pltpu.make_async_copy(w.at[:, :, u, :, :, pl.ds(MAIN, BLOCK - MAIN)], rest, local_sem.at[3])
        copy.start()
        copy.wait()
        for l in range(8):
            piece = rest[:, :, l // 2, l % 2].reshape(256, FFB)
            into[:, l * MAIN : (l + 1) * MAIN] = piece[:, :MAIN]

    def streamed(u, use):
        slabs(u, 0, 0).start()

        def two(i, carry):
            for j in range(2):
                now = 2 * i + j
                slabs(u, now, j).wait()

                @pl.when(now < 7)
                def _():
                    slabs(u, now + 1, 1 - j).start()

                use(now, j)
            return carry

        lax.fori_loop(0, 4, two, 0)

    sibling_finish(0)

    def up(now, slot):
        for j in range(2):
            product = jnp.dot(mixed[...], stage[slot, j].reshape(D, FFB), preferred_element_type=F32)
            hid[2 * now + j] = gelu(product + upb[2 * now + j]).astype(BF16)

    remainder(0, ru)
    streamed(0, up)
    product = lax.dot_general(mixed[...], ru[...], NT, preferred_element_type=F32)
    hid_r[...] = gelu(product + upb_rem[...]).astype(BF16)

    sibling_finish(1)

    def down(now, slot):
        total = None
        for j in range(2):
            part = lax.dot_general(hid[2 * now + j], stage[slot, j].reshape(D, FFB), NT, preferred_element_type=F32)
            total = part if total is None else total + part
        acc[...] += total

    remainder(1, rd)
    streamed(1, down)
    out[...] = (acc[...] + jnp.dot(hid_r[...], rd[...], preferred_element_type=F32)).astype(BF16)
    outer_sent()
    for copy in copies:
        copy.wait_send()


def per_device(
    tokens, lengths, norm_gains, norm_shifts, qkv_weight, qkv_bias, out_weight, out_bias, up_weight, up_bias,
    down_weight, down_bias,
):
    vmem = pl.BlockSpec(memory_space=pltpu.VMEM)
    hbm = pl.BlockSpec(memory_space=pl.ANY)
    dma = pltpu.SemaphoreType.DMA
    out, _ = pl.pallas_call(
        layer_kernel,
        out_shape=[
            jax.ShapeDtypeStruct((ROWS, D), BF16),
            jax.ShapeDtypeStruct((4, 4, 2, 4, 2, BLOCK, FFB), BF16),
        ],
        in_specs=[vmem, vmem, vmem, vmem, hbm, vmem, hbm, vmem, vmem, vmem, vmem, vmem],
        out_specs=[vmem, hbm],
        scratch_shapes=[
            pltpu.VMEM((2, BLOCK, FFB), BF16),
            pltpu.VMEM((FFB, FFB), F32),
            pltpu.VMEM((1, 3 * D), F32),
            pltpu.VMEM((1, D), F32),
            pltpu.VMEM((1, D), F32),
            pltpu.VMEM((16, 1, FFB), F32),
            pltpu.VMEM((1, 256), F32),
            pltpu.VMEM((4, 256, D), BF16),
            pltpu.VMEM((D, 3 * D), BF16),
            pltpu.VMEM((D, D), BF16),
            pltpu.VMEM((HEADS, ROWS, 128), BF16),
            pltpu.VMEM((HEADS, EXT, 128), BF16),
            pltpu.VMEM((HEADS, EXT, 128), BF16),
            pltpu.VMEM((ROWS, 128), BF16),
            pltpu.VMEM((EXT, 128), BF16),
            pltpu.VMEM((256, D), BF16),
            pltpu.VMEM((256, 3 * D), BF16),
            pltpu.VMEM((2, TILE, WINDOW), F32),
            pltpu.VMEM((2, TILE, 128), F32),
            pltpu.VMEM((ROWS, D), BF16),
            pltpu.VMEM((ROWS, D), F32),
            pltpu.VMEM((16, ROWS, FFB), BF16),
            pltpu.VMEM((ROWS, 256), BF16),
            pltpu.VMEM((2, 2, 4, 2, MAIN, FFB), BF16),
            pltpu.VMEM((4, 4, 4, 2, BLOCK - MAIN, FFB), BF16),
            pltpu.VMEM((256, D), BF16),
            pltpu.VMEM((256, D), BF16),
            dma((4,)),
            dma((2,)),
            dma((4,)),
            dma((4,)),
            dma((2, 3, 11)),
            dma((2, 3, 11)),
            dma((2, 3, 5)),
            dma((2, 3, 5)),
        ],
        compiler_params=pltpu.CompilerParams(
            collective_id=0, has_side_effects=True, vmem_limit_bytes=62 * 2**20
        ),
        cost_estimate=pl.CostEstimate(flops=40_000_000_000, bytes_accessed=50_000_000, transcendentals=20_000_000),
    )(
        tokens, lengths, norm_gains, norm_shifts, qkv_weight, qkv_bias, out_weight, out_bias, up_weight, up_bias,
        down_weight, down_bias,
    )
    return out


def solution(mesh):
    placed = (
        P(("loader", "encoder"), None),
        P("loader", None),
        P(),
        P(),
        P(),
        P(),
        P(),
        P(),
        P("loader", "encoder"),
        P(),
        P("encoder", "loader"),
        P(),
    )
    return jax.shard_map(
        per_device,
        mesh=mesh,
        in_specs=placed,
        out_specs=P(("loader", "encoder"), None),
        check_vma=False,
    )
```
